32 devices in a mesh: grp: 2 (over y), seq: 8 (over z, x), head: 2 (over core).
Axes of the slice: x: 2, y: 2, z: 4, core: 2. Of those that a mesh axis runs over, the one named last changes fastest.
Arguments:
- features: bfloat16 [8192, 2048], P(('grp', 'seq'), 'head'), parts along dimension 0, may hold values from -6 to 6
- keys_proj: bfloat16 [8192, 128], P(('grp', 'seq')), parts along dimension 0, may hold values from -0.5 to 0.5
- query_proj: bfloat16 [8192, 128], P(('grp', 'seq')), parts along dimension 0, may hold values from -0.5 to 0.5
- log_decay: float32 [32, 8192], P('head', ('grp', 'seq')), parts along dimension 1, may hold values from -1 to 0, as said below
- out_weight: bfloat16 [2048, 1024], P(None, 'head'), may hold values from -0.125 to 0.125
- out_grad: bfloat16 [8192, 1024], P(('grp', 'seq'), 'head'), parts along dimension 0, may hold values from -6 to 6
Outputs:
- grad_features: bfloat16 [8192, 2048], P(('grp', 'seq'), 'head'), parts along dimension 0
- grad_proj: float32 [2, 8192, 128], P('head', ('grp', 'seq')), parts along dimension 1
- grad_decay: float32 [32, 8192], P('head', ('grp', 'seq')), parts along dimension 1
The draws below stay inside these ranges and needn't reach their ends.
There are 2 independent parts, one for each index of `grp`. The reference program is written for one: setup_inputs(seed, part) draws one part's arguments, and reference() takes and returns one part's arrays. A program takes and returns all parts, laid end to end along the dimension named above; an argument that names none is the same for every part. Nothing has to cross between parts.
Inputs may be any that keep to these rules, and one draw needn't show every extreme that they name: log_decay is never positive.
All inputs are finite; a program needn't handle non-finite values.
Results may differ from the reference program's by a relative error of at most 0.0049.
Values may be sent and summed in bfloat16 or wider, within the bound.
A program may use at most 192 MiB of HBM per device.

```python
import jax
import jax.numpy as jnp
from jax import lax

D = 1024
HEAD_TOTAL = 32
P_SIZE = 64
N = 128
BLOCK = 256
TOK_DEV = 512
SCENE_TOKENS = 4096


def draw_log_decay(key, part):
    key = jax.random.fold_in(key, 7)
    streams = jax.random.split(key, 11)
    ranking = jax.random.permutation(streams[0], HEAD_TOTAL)
    steep_count = max(1, HEAD_TOTAL // 16)
    middle_count = max(1, HEAD_TOTAL // 8)
    fast_count = max(0, HEAD_TOTAL // 2 - steep_count - middle_count)
    is_steep = ranking < steep_count
    is_middle = (ranking >= steep_count) & (ranking < steep_count + middle_count)
    is_fast = (ranking >= steep_count + middle_count) & (ranking < steep_count + middle_count + fast_count)
    fast_rate = jnp.exp(jax.random.uniform(streams[1], (HEAD_TOTAL,), jnp.float32, jnp.log(1.0 / 50.0), jnp.log(1.0 / 30.0)))
    slow_rate = jnp.exp(jax.random.uniform(streams[2], (HEAD_TOTAL,), jnp.float32, jnp.log(0.1 / SCENE_TOKENS), jnp.log(0.5 / SCENE_TOKENS)))
    middle_rate = 5.0 / TOK_DEV * jnp.exp(jax.random.uniform(streams[8], (HEAD_TOTAL,), jnp.float32, jnp.log(0.8), jnp.log(1.25)))
    steep_rate = jax.random.uniform(streams[9], (HEAD_TOTAL,), jnp.float32, 0.5, 0.6)
    base_rate = jnp.where(is_fast, fast_rate, slow_rate)
    base_rate = jnp.where(is_middle, middle_rate, base_rate)
    base_rate = jnp.where(is_steep, steep_rate, base_rate)
    segments = SCENE_TOKENS // TOK_DEV
    wide_factor = jnp.exp(jax.random.uniform(streams[3], (HEAD_TOTAL, segments), jnp.float32, jnp.log(0.002), jnp.log(2.0)))
    narrow_factor = jnp.exp(jax.random.uniform(streams[10], (HEAD_TOTAL, segments), jnp.float32, jnp.log(0.8), jnp.log(1.25)))
    settled = (is_middle | is_steep)[:, None]
    block_factor = jnp.where(settled, narrow_factor, wide_factor)
    block_full = jnp.repeat(block_factor, TOK_DEV, axis=1)
    token_factor = jax.random.uniform(streams[4], (HEAD_TOTAL, SCENE_TOKENS), jnp.float32, 0.4, 1.6)
    log_rate_values = -(base_rate[:, None] * block_full * token_factor)
    half_length = SCENE_TOKENS // 2
    early_spot = jax.random.randint(streams[5], (HEAD_TOTAL, 1), 0, half_length)
    late_spot = jax.random.randint(streams[7], (HEAD_TOTAL, 1), half_length, SCENE_TOKENS)
    positions = jnp.concatenate([early_spot, late_spot], axis=1)
    discard_size = jax.random.uniform(streams[6], (HEAD_TOTAL, 2), jnp.float32, jnp.log(0.5), jnp.log(0.8))
    rows_per_head = jnp.arange(HEAD_TOTAL)[:, None] * jnp.ones((1, 2), jnp.int32)
    spike_terms = jnp.zeros((HEAD_TOTAL, SCENE_TOKENS), jnp.float32).at[rows_per_head, positions].add(discard_size)
    return jnp.maximum(log_rate_values + spike_terms, -1.0).astype(jnp.float32)


def draw_features(key, part):
    key = jax.random.fold_in(key, 11)
    streams = jax.random.split(key, 2)
    segments = SCENE_TOKENS // TOK_DEV
    shape = (SCENE_TOKENS, HEAD_TOTAL * P_SIZE)
    base = jnp.clip(jax.random.normal(streams[0], shape, jnp.float32), -6.0, 6.0)
    level = jnp.exp(jax.random.uniform(streams[1], (segments, HEAD_TOTAL), jnp.float32, -3.5, 0.0))
    shaped = base.reshape(segments, TOK_DEV, HEAD_TOTAL, P_SIZE) * level[:, None, :, None]
    return shaped.reshape(SCENE_TOKENS, HEAD_TOTAL * P_SIZE).astype(jnp.bfloat16)


def draw_out_grad(key, part):
    key = jax.random.fold_in(key, 13)
    streams = jax.random.split(key, 2)
    segments = SCENE_TOKENS // TOK_DEV
    shape = (SCENE_TOKENS, D)
    base = jnp.clip(jax.random.normal(streams[0], shape, jnp.float32), -6.0, 6.0)
    level = jnp.exp(jax.random.uniform(streams[1], (segments,), jnp.float32, -3.5, 0.0))
    shaped = base.reshape(segments, TOK_DEV, D) * level[:, None, None]
    return shaped.reshape(SCENE_TOKENS, D).astype(jnp.bfloat16)


def steps_of(own_key, dims, shards, least, largest):
    def one(position, shards_of):
        heights = jax.random.uniform(jax.random.fold_in(jax.random.fold_in(own_key, 6), position), (shards_of,), jnp.float32, least / len(shards), largest / len(shards))
        return jnp.repeat(jnp.exp(heights), dims[position] // shards_of).reshape((-1,) + (1,) * (len(dims) - position - 1))

    loudness = one(*shards[0])
    for cut in shards[1:]:
        loudness = loudness * one(*cut)
    return loudness


def noise(key, dims, width, bound, shards=(), held_as=jnp.bfloat16):
    drawn = jax.random.normal(key, dims, jnp.float32) * width
    if len(shards) > 0:
        drawn = steps_of(key, dims, shards, -0.22, 0.18) * drawn
    return jnp.clip(drawn, min=-bound, max=bound).astype(held_as)


def setup_inputs(seed: int = 0, part: int = 0) -> dict:
    arg_keys = jax.random.split(jax.random.key(seed), 7)
    part_keys = jax.random.split(jax.random.fold_in(arg_keys[6], part), 7)
    return {
        "features": draw_features(jax.random.fold_in(jax.random.fold_in(arg_keys[6], part), 71), part),
        "keys_proj": noise(part_keys[1], (SCENE_TOKENS, N), ((N * SCENE_TOKENS) ** -0.25), 0.5, ((0, 8),)),
        "query_proj": noise(part_keys[2], (SCENE_TOKENS, N), ((N * SCENE_TOKENS) ** -0.25), 0.5, ((0, 8),)),
        "log_decay": draw_log_decay(jax.random.fold_in(jax.random.fold_in(arg_keys[6], part), 71), part),
        "out_weight": noise(arg_keys[4], (HEAD_TOTAL * P_SIZE, D), (HEAD_TOTAL * P_SIZE) ** -0.5, 0.125, ((1, 2),)),
        "out_grad": draw_out_grad(jax.random.fold_in(jax.random.fold_in(arg_keys[6], part), 71), part),
    }


highest = lax.Precision.HIGHEST


def decay_tables(cumulative):
    length = cumulative.shape[-1]
    row_index = lax.broadcasted_iota(jnp.int32, (length, length), 0)
    col_index = lax.broadcasted_iota(jnp.int32, (length, length), 1)
    causal = row_index >= col_index
    log_gap = cumulative[..., :, None] - cumulative[..., None, :]
    within = jnp.where(causal, jnp.exp(jnp.where(causal, log_gap, 0.0)), 0.0)
    tail_decay = jnp.exp(cumulative[..., -1:] - cumulative)
    return within, tail_decay


def reference(features, keys_proj, query_proj, log_decay, out_weight, out_grad):
    token_total, inner_width = features.shape
    head_count = log_decay.shape[0]
    head_size = inner_width // head_count
    state_size = keys_proj.shape[1]
    block_count = token_total // BLOCK
    grad_output = jnp.dot(out_grad, out_weight.T, preferred_element_type=jnp.float32).astype(jnp.bfloat16)
    feature_blocks = features.reshape(block_count, BLOCK, head_count, head_size)
    key_blocks = keys_proj.reshape(block_count, BLOCK, state_size)
    query_blocks = query_proj.reshape(block_count, BLOCK, state_size)
    rate_blocks = jnp.transpose(log_decay.reshape(head_count, block_count, BLOCK), (1, 0, 2))
    grad_blocks = grad_output.reshape(block_count, BLOCK, head_count, head_size)
    zero_state = jnp.zeros((head_count, head_size, state_size), jnp.float32)

    def forward(carried, pieces):
        feat_here, keys_here, query_here, rate_here = pieces
        cumulative = jnp.cumsum(rate_here, axis=-1)
        within, tail_decay = decay_tables(cumulative)
        scores = jnp.dot(query_here, keys_here.T, preferred_element_type=jnp.float32)
        weights = within * scores[None]
        feat_float = feat_here.astype(jnp.float32)
        key_float = keys_here.astype(jnp.float32)
        query_float = query_here.astype(jnp.float32)
        local_part = jnp.einsum("hij,jhp->ihp", weights, feat_float, precision=highest)
        carried_part = jnp.einsum("in,hpn->ihp", query_float, carried, precision=highest) * jnp.exp(cumulative).T[:, :, None]
        fresh_state = jnp.einsum("jhp,hjn->hpn", feat_float, tail_decay[:, :, None] * key_float[None], precision=highest)
        factor = jnp.exp(cumulative[:, -1])
        return factor[:, None, None] * carried + fresh_state, (local_part + carried_part, carried)

    _, (outputs, starts) = lax.scan(forward, zero_state, (feature_blocks, key_blocks, query_blocks, rate_blocks))

    def backward(adjoint, pieces):
        grad_here, query_here, rate_here = pieces
        cumulative = jnp.cumsum(rate_here, axis=-1)
        growth = jnp.exp(cumulative)
        upward = jnp.einsum("ihp,hin->hpn", grad_here.astype(jnp.float32), growth[:, :, None] * query_here.astype(jnp.float32)[None], precision=highest)
        return upward + growth[:, -1][:, None, None] * adjoint, adjoint

    _, adjoints = lax.scan(backward, zero_state, (grad_blocks, query_blocks, rate_blocks), reverse=True)

    def local_terms(pieces):
        feat_here, keys_here, query_here, rate_here, grad_here, output, state_start, adjoint = pieces
        cumulative = jnp.cumsum(rate_here, axis=-1)
        within, tail_decay = decay_tables(cumulative)
        growth = jnp.exp(cumulative)
        scores = jnp.dot(query_here, keys_here.T, preferred_element_type=jnp.float32)
        weights = within * scores[None]
        feat_float = feat_here.astype(jnp.float32)
        key_float = keys_here.astype(jnp.float32)
        query_float = query_here.astype(jnp.float32)
        grad_float = grad_here.astype(jnp.float32)
        grad_in = jnp.einsum("hij,ihp->jhp", weights, grad_float, precision=highest) + jnp.einsum("jn,hpn->jhp", key_float, adjoint, precision=highest) * tail_decay.T[:, :, None]
        mixed_scores = jnp.einsum("ihp,jhp->hij", grad_float, feat_float, precision=highest)
        decayed_mix = within * mixed_scores
        grad_keys = jnp.einsum("hij,in->jn", decayed_mix, query_float, precision=highest) + jnp.einsum("jhp,hpn,hj->jn", feat_float, adjoint, tail_decay, precision=highest)
        grad_query = jnp.einsum("hij,jn->in", decayed_mix, key_float, precision=highest) + jnp.einsum("ihp,hpn,hi->in", grad_float, state_start, growth, precision=highest)
        mismatch = jnp.sum(grad_float * output, axis=2) - jnp.sum(feat_float * grad_in, axis=2)
        return grad_in, grad_keys, grad_query, mismatch

    grad_in, grad_keys, grad_query, mismatch = lax.map(local_terms, (feature_blocks, key_blocks, query_blocks, rate_blocks, grad_blocks, outputs, starts, adjoints))
    flat_terms = jnp.transpose(mismatch.reshape(token_total, head_count))
    grad_decay = jnp.flip(jnp.cumsum(jnp.flip(flat_terms, 1), axis=1), 1)
    grad_features = grad_in.reshape(token_total, inner_width).astype(jnp.bfloat16)
    grad_proj = jnp.stack([grad_keys.reshape(token_total, state_size), grad_query.reshape(token_total, state_size)])
    return grad_features, grad_proj, grad_decay
```

```python
import functools

import jax
import jax.numpy as jnp
from jax import lax
from jax.experimental import pallas as pl
from jax.experimental.pallas import tpu as pltpu
from jax.sharding import PartitionSpec as P

BLOCK = 256
F32 = jnp.float32
BF16 = jnp.bfloat16
MESH = pl.DeviceIdType.MESH


def nn(a, b, **kw):
    return lax.dot_general(a, b, (((1,), (0,)), ((), ())), preferred_element_type=F32, **kw)


def nt(a, b, **kw):
    return lax.dot_general(a, b, (((1,), (1,)), ((), ())), preferred_element_type=F32, **kw)


def tn(a, b, **kw):
    return lax.dot_general(a, b, (((0,), (0,)), ((), ())), preferred_element_type=F32, **kw)


def kernel(
    n, heads, hs, blocks,
    f_ref, k_ref, q_ref, ld_ref, w_ref, og_ref,
    gf_ref, gp_ref, gd_ref,
    w_in, og_in, gp_in, gp_stage, tot,
    stage, pair_in, half, z_in, ret_out, ret_in,
    a_ref, ac_ref, xt, xs, gt, gs, gi, fresh, up, local, enter, mis, mixsum, scm,
    hd_send, hd_recv, tot_send, tot_recv, pr_send, pr_recv, z_send, z_recv,
):
    me = lax.axis_index("seq")
    hd = lax.axis_index("head")
    other = 1 - hd
    pairs = n // 2
    pair = me // 2
    par = lax.rem(me, 2)
    mate = me + 1 - 2 * par
    inner = heads * hs
    hh = heads // 2
    hrows = inner // 2
    tokens = blocks * BLOCK

    barrier = pltpu.get_barrier_semaphore()
    pl.semaphore_signal(barrier, inc=1, device_id={"head": other}, device_id_type=MESH)

    def greet(j, c):
        @pl.when(j != me)
        def _():
            pl.semaphore_signal(barrier, inc=1, device_id={"seq": j}, device_id_type=MESH)
        return c

    lax.fori_loop(0, n, greet, 0)
    pl.semaphore_wait(barrier, n)

    def to_head(src, dst, i):
        return pltpu.make_async_remote_copy(
            src_ref=src, dst_ref=dst, send_sem=hd_send.at[i], recv_sem=hd_recv.at[i],
            device_id={"head": other}, device_id_type=MESH)

    send_og = to_head(og_ref, og_in, 0)
    send_w = to_head(w_ref.at[pl.ds(pl.multiple_of(other * inner, inner), inner), :], w_in, 1)
    send_og.start()
    send_w.start()

    rows = lax.broadcasted_iota(jnp.int32, (BLOCK, BLOCK), 0)
    cols = lax.broadcasted_iota(jnp.int32, (BLOCK, BLOCK), 1)
    upper = (rows <= cols).astype(F32)
    hi = lax.Precision.HIGHEST
    lasts = []
    for b in range(blocks):
        ld = ld_ref[:, b * BLOCK:(b + 1) * BLOCK]
        a = nn(ld, upper, precision=hi)
        at = lax.dot_general(upper, ld, (((0,), (1,)), ((), ())), preferred_element_type=F32, precision=hi)
        a_ref[b] = a
        for h in range(heads):
            ac_ref[b, h] = at[:, h:h + 1]
        lasts.append(jnp.broadcast_to(a[:, BLOCK - 1:BLOCK], (heads, 128)))
    total = lasts[0]
    for b in range(1, blocks):
        total = total + lasts[b]
    e = [jnp.exp(v) for v in lasts]
    tot[me] = total

    def tot_copy(j):
        return pltpu.make_async_remote_copy(
            src_ref=tot.at[me], dst_ref=tot.at[me], send_sem=tot_send.at[j], recv_sem=tot_recv.at[me],
            device_id={"seq": j}, device_id_type=MESH)

    def tot_go(j, c):
        @pl.when(j != me)
        def _():
            tot_copy(j).start()
        return c

    lax.fori_loop(0, n, tot_go, 0)

    for b in range(blocks):
        xt[b] = f_ref[b * BLOCK:(b + 1) * BLOCK, :].T
        for h in range(heads):
            r = slice(h * hs, (h + 1) * hs)
            arow = a_ref[b, h:h + 1, :]
            tail = jnp.exp(arow[:, BLOCK - 1:BLOCK] - arow)
            xs[b, r, :] = (xt[b, r, :].astype(F32) * tail).astype(BF16)
        fresh[b] = nn(xs[b], k_ref[b * BLOCK:(b + 1) * BLOCK, :])
    for h in range(heads):
        r = slice(h * hs, (h + 1) * hs)
        s = fresh[0, r, :]
        for b in range(1, blocks):
            s = e[b][h:h + 1, :] * s + fresh[b, r, :]
        local[0, r, :] = s
        stage[0, r, :] = s.astype(BF16)

    mine_rows = pl.ds(pl.multiple_of(par * hrows, hrows), hrows)
    mate_rows = pl.ds(pl.multiple_of((1 - par) * hrows, hrows), hrows)

    def to_mate(src, dst, i):
        return pltpu.make_async_remote_copy(
            src_ref=src, dst_ref=dst, send_sem=pr_send.at[i], recv_sem=pr_recv.at[i],
            device_id={"seq": mate}, device_id_type=MESH)

    pair_f = to_mate(stage.at[0, mate_rows, :], pair_in.at[0], 0)
    pair_f.start()

    for b in range(blocks):
        t = slice(b * BLOCK, (b + 1) * BLOCK)
        scm[b] = jnp.where(rows >= cols, nt(q_ref[t, :], k_ref[t, :]), 0.0)
        mixsum[b] = jnp.zeros((BLOCK, BLOCK), F32)

    send_og.wait_recv()
    send_w.wait_recv()
    chunk = 8 * hs

    def g_step(i, c):
        r0 = pl.multiple_of(i * chunk, chunk)
        w_own = w_ref[pl.ds(pl.multiple_of(hd * inner + r0, chunk), chunk), :]
        g = nt(w_own, og_ref[...]) + nt(w_in[pl.ds(r0, chunk), :], og_in[...])
        g = g.astype(BF16)
        for b in range(blocks):
            gb = g[:, b * BLOCK:(b + 1) * BLOCK]
            gt[b, pl.ds(r0, chunk), :] = gb
            growth = jnp.exp(a_ref[b, pl.ds(pl.multiple_of(i * 8, 8), 8), :])
            for m in range(8):
                gs[b, pl.ds(pl.multiple_of(r0 + m * hs, hs), hs), :] = (
                    gb[m * hs:(m + 1) * hs, :].astype(F32) * growth[m:m + 1, :]).astype(BF16)
        return c

    lax.fori_loop(0, heads // 8, g_step, 0)
    for b in range(blocks):
        up[b] = nn(gs[b], q_ref[b * BLOCK:(b + 1) * BLOCK, :])
    for h in range(heads):
        r = slice(h * hs, (h + 1) * hs)
        s = up[blocks - 1, r, :]
        for b in reversed(range(blocks - 1)):
            s = e[b][h:h + 1, :] * s + up[b, r, :]
        local[1, r, :] = s
        stage[1, r, :] = s.astype(BF16)
    pair_b = to_mate(stage.at[1, mate_rows, :], pair_in.at[1], 1)
    pair_b.start()

    def tot_wait(j, c):
        @pl.when(j != me)
        def _():
            pltpu.make_async_remote_copy(
                src_ref=tot.at[j], dst_ref=tot.at[j], send_sem=tot_send.at[j], recv_sem=tot_recv.at[j],
                device_id={"seq": j}, device_id_type=MESH).wait_recv()
        return c

    lax.fori_loop(0, n, tot_wait, 0)
    e_lo = jnp.exp(tot[2 * pair, pl.ds(pl.multiple_of(par * hh, hh), hh), :])
    e_hi = jnp.exp(tot[2 * pair + 1, pl.ds(pl.multiple_of(par * hh, hh), hh), :])
    is_lo = par == 0

    def z_copy(d, zz):
        return pltpu.make_async_remote_copy(
            src_ref=half.at[d], dst_ref=z_in.at[d, pair],
            send_sem=z_send.at[d, zz], recv_sem=z_recv.at[d, pair],
            device_id={"seq": 2 * zz + par}, device_id_type=MESH)

    def sides(d, h):
        own = local[d, pl.ds(pl.multiple_of(par * hrows + h * hs, hs), hs), :]
        got = pair_in[d, h * hs:(h + 1) * hs, :].astype(F32)
        return jnp.where(is_lo, own, got), jnp.where(is_lo, got, own)

    pair_f.wait_recv()
    for h in range(hh):
        lo, high = sides(0, h)
        half[0, h * hs:(h + 1) * hs, :] = (e_hi[h:h + 1, :] * lo + high).astype(BF16)

    def z_go(d, zz):
        @pl.when(zz > pair if d == 0 else zz < pair)
        def _():
            z_copy(d, zz).start()

    def z_each(d, act):
        def run(zz, c):
            @pl.when(zz > pair if d == 0 else zz < pair)
            def _():
                act(z_copy(d, zz))
            return c
        lax.fori_loop(0, pairs, run, 0)

    z_each(0, lambda c: c.start())
    pair_b.wait_recv()
    for h in range(hh):
        lo, high = sides(1, h)
        half[1, h * hs:(h + 1) * hs, :] = (e_lo[h:h + 1, :] * high + lo).astype(BF16)
    z_each(1, lambda c: c.start())

    def head_step(h, c):
        r = pl.ds(pl.multiple_of(h * hs, hs), hs)
        for b in range(blocks):
            gap = jnp.minimum(ac_ref[b, h] - a_ref[b, pl.ds(h, 1), :], 0.0)
            within = jnp.exp(gap)
            gh = gt[b, r, :]
            xh = xt[b, r, :]
            mixsum[b] += within * tn(gh, xh)
            weights = (within * scm[b]).astype(BF16)
            y = nt(xh, weights)
            gin = nn(gh, weights)
            gi[b, r, :] = gin
            mis[b, pl.ds(h, 1), :] = jnp.sum(gh.astype(F32) * y - xh.astype(F32) * gin, axis=0, keepdims=True)
        return c

    lax.fori_loop(0, heads, head_step, 0)

    enter[:, mine_rows, :] = jnp.zeros((2, hrows, 128), F32)
    half_heads = pl.ds(pl.multiple_of(par * hh, hh), hh)
    for d in range(2):
        def gather(step, c, d=d):
            zz = step if d == 0 else pairs - 1 - step

            @pl.when(zz < pair if d == 0 else zz > pair)
            def _():
                pltpu.make_async_remote_copy(
                    src_ref=half.at[d], dst_ref=z_in.at[d, zz],
                    send_sem=z_send.at[d, zz], recv_sem=z_recv.at[d, zz],
                    device_id={"seq": 2 * zz + par}, device_id_type=MESH).wait_recv()
                ez = jnp.exp(tot[2 * zz, half_heads, :] + tot[2 * zz + 1, half_heads, :])
                for h in range(hh):
                    r = pl.ds(pl.multiple_of(par * hrows + h * hs, hs), hs)
                    enter[d, r, :] = ez[h:h + 1, :] * enter[d, r, :] + z_in[d, zz, h * hs:(h + 1) * hs, :].astype(F32)
            return c

        lax.fori_loop(0, pairs, gather, 0)
    rets = []
    for d in range(2):
        for h in range(hh):
            r = pl.ds(pl.multiple_of(par * hrows + h * hs, hs), hs)
            lo, high = sides(d, h)
            base = enter[d, r, :]
            if d == 0:
                far = e_lo[h:h + 1, :] * base + lo
                far_mine = par == 1
            else:
                far = e_hi[h:h + 1, :] * base + high
                far_mine = par == 0
            enter[d, r, :] = jnp.where(far_mine, far, base)
            ret_out[d, h * hs:(h + 1) * hs, :] = jnp.where(far_mine, base, far).astype(BF16)
        c = to_mate(ret_out.at[d], ret_in.at[d], 2 + d)
        c.start()
        rets.append(c)
    for d in range(2):
        rets[d].wait_recv()
        enter[d, mate_rows, :] = ret_in[d].astype(F32)

    for h in range(heads):
        r = slice(h * hs, (h + 1) * hs)
        states = [enter[0, r, :]]
        for b in range(blocks):
            states.append(e[b][h:h + 1, :] * states[b] + fresh[b, r, :])
        adj = enter[1, r, :]
        for b in reversed(range(blocks)):
            nxt = e[b][h:h + 1, :] * adj + up[b, r, :]
            base = jnp.sum(jnp.sum(states[b + 1] * adj, axis=0, keepdims=True), axis=1, keepdims=True)
            gd_ref[h:h + 1, b * BLOCK:(b + 1) * BLOCK] = jnp.broadcast_to(base, (1, BLOCK))
            up[b, r, :] = adj
            adj = nxt
        for b in range(blocks):
            fresh[b, r, :] = states[b]
    lower = (rows >= cols).astype(F32)
    for b in range(blocks):
        t = slice(b * BLOCK, (b + 1) * BLOCK)
        kb = k_ref[t, :]
        qb = q_ref[t, :]
        sb = fresh[b].astype(BF16)
        ab = up[b].astype(BF16)
        mixed = jnp.where(rows >= cols, mixsum[b], 0.0).astype(BF16)
        gp_stage[0, t, :] = tn(mixed, qb) + tn(xs[b], ab)
        gp_stage[1, t, :] = nn(mixed, kb) + tn(gs[b], sb)
    send_gp = to_head(gp_stage.at[other], gp_in, 2)
    send_gp.start()
    for b in range(blocks):
        t = slice(b * BLOCK, (b + 1) * BLOCK)
        kb = k_ref[t, :]
        qb = q_ref[t, :]
        for h in range(heads):
            r = slice(h * hs, (h + 1) * hs)
            arow = a_ref[b, h:h + 1, :]
            tail = jnp.exp(arow[:, BLOCK - 1:BLOCK] - arow)
            growth = jnp.exp(arow)
            yc = nt(fresh[b, r, :].astype(BF16), qb)
            gc = nt(up[b, r, :].astype(BF16), kb) * tail
            gi[b, r, :] += gc
            mis[b, h:h + 1, :] += (
                jnp.sum(gt[b, r, :].astype(F32) * yc, axis=0, keepdims=True) * growth
                - jnp.sum(xt[b, r, :].astype(F32) * gc, axis=0, keepdims=True))
        gf_ref[t, :] = gi[b].astype(BF16).T
        gd_ref[:, t] += nn(mis[b], lower, precision=hi)
    send_gp.wait_recv()
    gp_ref[0] = gp_stage[hd] + gp_in[...]

    send_og.wait_send()
    send_w.wait_send()
    send_gp.wait_send()
    pair_f.wait_send()
    pair_b.wait_send()
    for d in range(2):
        rets[d].wait_send()
        z_each(d, lambda c: c.wait_send())

    def tot_done(j, c):
        @pl.when(j != me)
        def _():
            tot_copy(j).wait_send()
        return c

    lax.fori_loop(0, n, tot_done, 0)


def body(n, features, keys_proj, query_proj, log_decay, out_weight, out_grad):
    tokens, inner = features.shape
    heads = log_decay.shape[0]
    hs = inner // heads
    ns = keys_proj.shape[1]
    depth = out_grad.shape[1]
    blocks = tokens // BLOCK
    pairs = n // 2
    half = inner // 2
    vm = pltpu.VMEM
    dma = pltpu.SemaphoreType.DMA
    scratch = [
        vm((inner, depth), BF16), vm((tokens, depth), BF16), vm((tokens, ns), F32),
        vm((2, tokens, ns), F32), vm((n, heads, 128), F32),
        vm((2, inner, ns), BF16), vm((2, half, ns), BF16), vm((2, half, ns), BF16),
        vm((2, pairs, half, ns), BF16), vm((2, half, ns), BF16), vm((2, half, ns), BF16),
        vm((blocks, heads, BLOCK), F32), vm((blocks, heads, BLOCK, 1), F32),
        vm((blocks, inner, BLOCK), BF16), vm((blocks, inner, BLOCK), BF16),
        vm((blocks, inner, BLOCK), BF16), vm((blocks, inner, BLOCK), BF16),
        vm((blocks, inner, BLOCK), F32),
        vm((blocks, inner, ns), F32), vm((blocks, inner, ns), F32),
        vm((2, inner, ns), F32), vm((2, inner, ns), F32),
        vm((blocks, heads, BLOCK), F32), vm((blocks, BLOCK, BLOCK), F32), vm((blocks, BLOCK, BLOCK), F32),
        dma((3,)), dma((3,)), dma((n,)), dma((n,)), dma((4,)), dma((4,)),
        dma((2, pairs)), dma((2, pairs)),
    ]
    spec = pl.BlockSpec(memory_space=pltpu.VMEM)
    return pl.pallas_call(
        functools.partial(kernel, n, heads, hs, blocks),
        out_shape=(
            jax.ShapeDtypeStruct((tokens, inner), BF16),
            jax.ShapeDtypeStruct((1, tokens, ns), F32),
            jax.ShapeDtypeStruct((heads, tokens), F32),
        ),
        in_specs=[spec] * 6,
        out_specs=(spec,) * 3,
        scratch_shapes=scratch,
        compiler_params=pltpu.CompilerParams(
            collective_id=0, has_side_effects=True, vmem_limit_bytes=56 * 1024 * 1024),
    )(features, keys_proj, query_proj, log_decay, out_weight, out_grad)


def solution(mesh):
    placed = (
        P(("grp", "seq"), "head"),
        P(("grp", "seq"), None),
        P(("grp", "seq"), None),
        P("head", ("grp", "seq")),
        P(None, "head"),
        P(("grp", "seq"), "head"),
    )
    return jax.shard_map(
        functools.partial(body, mesh.shape["seq"]),
        mesh=mesh,
        in_specs=placed,
        out_specs=(
            P(("grp", "seq"), "head"),
            P("head", ("grp", "seq"), None),
            P("head", ("grp", "seq")),
        ),
        check_vma=False,
    )
```

```python
import functools

import jax
import jax.numpy as jnp
from jax import lax
from jax.experimental import pallas as pl
from jax.experimental.pallas import tpu as pltpu
from jax.sharding import PartitionSpec as P

BLOCK = 256
F32 = jnp.float32
BF16 = jnp.bfloat16
MESH = pl.DeviceIdType.MESH


def nn(a, b, **kw):
    return lax.dot_general(a, b, (((1,), (0,)), ((), ())), preferred_element_type=F32, **kw)


def nt(a, b, **kw):
    return lax.dot_general(a, b, (((1,), (1,)), ((), ())), preferred_element_type=F32, **kw)


def tn(a, b, **kw):
    return lax.dot_general(a, b, (((0,), (0,)), ((), ())), preferred_element_type=F32, **kw)


def kernel(
    n, heads, hs, blocks,
    f_ref, k_ref, q_ref, ld_ref, w_ref, og_ref,
    gf_ref, gp_ref, gd_ref,
    w_in, og_in, gp_in, gp_stage, tot,
    stage, pair_in, half, z_in, ret_out, ret_in,
    a_ref, ac_ref, xt, xs, gt, gs, gi, fresh, up, local, enter, mis, mixsum, scm,
    hd_send, hd_recv, tot_send, tot_recv, pr_send, pr_recv, z_send, z_recv,
):
    me = lax.axis_index("seq")
    hd = lax.axis_index("head")
    other = 1 - hd
    pairs = n // 2
    pair = me // 2
    par = lax.rem(me, 2)
    mate = me + 1 - 2 * par
    inner = heads * hs
    hh = heads // 2
    hrows = inner // 2
    tokens = blocks * BLOCK

    barrier = pltpu.get_barrier_semaphore()
    pl.semaphore_signal(barrier, inc=1, device_id={"head": other}, device_id_type=MESH)

    def greet(j, c):
        @pl.when(j != me)
        def _():
            pl.semaphore_signal(barrier, inc=1, device_id={"seq": j}, device_id_type=MESH)
        return c

    lax.fori_loop(0, n, greet, 0)
    pl.semaphore_wait(barrier, n)

    def to_head(src, dst, i):
        return pltpu.make_async_remote_copy(
            src_ref=src, dst_ref=dst, send_sem=hd_send.at[i], recv_sem=hd_recv.at[i],
            device_id={"head": other}, device_id_type=MESH)

    send_og = to_head(og_ref, og_in, 0)
    send_w = to_head(w_ref.at[pl.ds(pl.multiple_of(other * inner, inner), inner), :], w_in, 1)
    send_og.start()
    send_w.start()

    rows = lax.broadcasted_iota(jnp.int32, (BLOCK, BLOCK), 0)
    cols = lax.broadcasted_iota(jnp.int32, (BLOCK, BLOCK), 1)
    upper = (rows <= cols).astype(F32)
    hi = lax.Precision.HIGHEST
    lasts = []
    for b in range(blocks):
        ld = ld_ref[:, b * BLOCK:(b + 1) * BLOCK]
        a = nn(ld, upper, precision=hi)
        a_ref[b] = a
        lasts.append(jnp.broadcast_to(a[:, BLOCK - 1:BLOCK], (heads, 128)))
    total = lasts[0]
    for b in range(1, blocks):
        total = total + lasts[b]
    e = [jnp.exp(v) for v in lasts]
    tot[me] = total

    def tot_copy(j):
        return pltpu.make_async_remote_copy(
            src_ref=tot.at[me], dst_ref=tot.at[me], send_sem=tot_send.at[j], recv_sem=tot_recv.at[me],
            device_id={"seq": j}, device_id_type=MESH)

    def tot_go(j, c):
        @pl.when(j != me)
        def _():
            tot_copy(j).start()
        return c

    lax.fori_loop(0, n, tot_go, 0)

    for b in range(blocks):
        xt[b] = f_ref[b * BLOCK:(b + 1) * BLOCK, :].T
        for h in range(heads):
            r = slice(h * hs, (h + 1) * hs)
            arow = a_ref[b, h:h + 1, :]
            tail = jnp.exp(arow[:, BLOCK - 1:BLOCK] - arow)
            xs[b, r, :] = (xt[b, r, :].astype(F32) * tail).astype(BF16)
        fresh[b] = nn(xs[b], k_ref[b * BLOCK:(b + 1) * BLOCK, :])
    for h in range(heads):
        r = slice(h * hs, (h + 1) * hs)
        s = fresh[0, r, :]
        for b in range(1, blocks):
            s = e[b][h:h + 1, :] * s + fresh[b, r, :]
        local[0, r, :] = s
        stage[0, r, :] = s.astype(BF16)

    mine_rows = pl.ds(pl.multiple_of(par * hrows, hrows), hrows)
    mate_rows = pl.ds(pl.multiple_of((1 - par) * hrows, hrows), hrows)

    def to_mate(src, dst, i):
        return pltpu.make_async_remote_copy(
            src_ref=src, dst_ref=dst, send_sem=pr_send.at[i], recv_sem=pr_recv.at[i],
            device_id={"seq": mate}, device_id_type=MESH)

    pair_f = to_mate(stage.at[0, mate_rows, :], pair_in.at[0], 0)
    pair_f.start()

    send_og.wait_recv()
    send_w.wait_recv()
    chunk = 8 * hs

    def g_step(i, c):
        r0 = pl.multiple_of(i * chunk, chunk)
        w_own = w_ref[pl.ds(pl.multiple_of(hd * inner + r0, chunk), chunk), :]
        g = nt(w_own, og_ref[...]) + nt(w_in[pl.ds(r0, chunk), :], og_in[...])
        g = g.astype(BF16)
        for b in range(blocks):
            gb = g[:, b * BLOCK:(b + 1) * BLOCK]
            gt[b, pl.ds(r0, chunk), :] = gb
            growth = jnp.exp(a_ref[b, pl.ds(pl.multiple_of(i * 8, 8), 8), :])
            for m in range(8):
                gs[b, pl.ds(pl.multiple_of(r0 + m * hs, hs), hs), :] = (
                    gb[m * hs:(m + 1) * hs, :].astype(F32) * growth[m:m + 1, :]).astype(BF16)
        return c

    lax.fori_loop(0, heads // 8, g_step, 0)
    for b in range(blocks):
        up[b] = nn(gs[b], q_ref[b * BLOCK:(b + 1) * BLOCK, :])
    for h in range(heads):
        r = slice(h * hs, (h + 1) * hs)
        s = up[blocks - 1, r, :]
        for b in reversed(range(blocks - 1)):
            s = e[b][h:h + 1, :] * s + up[b, r, :]
        local[1, r, :] = s
        stage[1, r, :] = s.astype(BF16)
    pair_b = to_mate(stage.at[1, mate_rows, :], pair_in.at[1], 1)
    pair_b.start()

    def tot_wait(j, c):
        @pl.when(j != me)
        def _():
            pltpu.make_async_remote_copy(
                src_ref=tot.at[j], dst_ref=tot.at[j], send_sem=tot_send.at[j], recv_sem=tot_recv.at[j],
                device_id={"seq": j}, device_id_type=MESH).wait_recv()
        return c

    lax.fori_loop(0, n, tot_wait, 0)
    e_lo = jnp.exp(tot[2 * pair, pl.ds(pl.multiple_of(par * hh, hh), hh), :])
    e_hi = jnp.exp(tot[2 * pair + 1, pl.ds(pl.multiple_of(par * hh, hh), hh), :])
    is_lo = par == 0

    def z_copy(d, zz):
        return pltpu.make_async_remote_copy(
            src_ref=half.at[d], dst_ref=z_in.at[d, pair],
            send_sem=z_send.at[d, zz], recv_sem=z_recv.at[d, pair],
            device_id={"seq": 2 * zz + par}, device_id_type=MESH)

    def sides(d, h):
        own = local[d, pl.ds(pl.multiple_of(par * hrows + h * hs, hs), hs), :]
        got = pair_in[d, h * hs:(h + 1) * hs, :].astype(F32)
        return jnp.where(is_lo, own, got), jnp.where(is_lo, got, own)

    pair_f.wait_recv()
    for h in range(hh):
        lo, high = sides(0, h)
        half[0, h * hs:(h + 1) * hs, :] = (e_hi[h:h + 1, :] * lo + high).astype(BF16)

    def z_go(d, zz):
        @pl.when(zz > pair if d == 0 else zz < pair)
        def _():
            z_copy(d, zz).start()

    def z_each(d, act):
        def run(zz, c):
            @pl.when(zz > pair if d == 0 else zz < pair)
            def _():
                act(z_copy(d, zz))
            return c
        lax.fori_loop(0, pairs, run, 0)

    z_each(0, lambda c: c.start())

    for b in range(blocks):
        t = slice(b * BLOCK, (b + 1) * BLOCK)
        scm[b] = jnp.where(rows >= cols, nt(q_ref[t, :], k_ref[t, :]), 0.0)
        mixsum[b] = jnp.zeros((BLOCK, BLOCK), F32)
        at = lax.dot_general(upper, ld_ref[:, t], (((0,), (1,)), ((), ())), preferred_element_type=F32, precision=hi)
        for h in range(heads):
            ac_ref[b, h] = at[:, h:h + 1]

    pair_b.wait_recv()
    for h in range(hh):
        lo, high = sides(1, h)
        half[1, h * hs:(h + 1) * hs, :] = (e_lo[h:h + 1, :] * high + lo).astype(BF16)
    z_each(1, lambda c: c.start())

    def head_step(h, c):
        r = pl.ds(pl.multiple_of(h * hs, hs), hs)
        for b in range(blocks):
            gap = jnp.minimum(ac_ref[b, h] - a_ref[b, pl.ds(h, 1), :], 0.0)
            within = jnp.exp(gap)
            gh = gt[b, r, :]
            xh = xt[b, r, :]
            mixsum[b] += within * tn(gh, xh)
            weights = (within * scm[b]).astype(BF16)
            y = nt(xh, weights)
            gin = nn(gh, weights)
            gi[b, r, :] = gin
            mis[b, pl.ds(h, 1), :] = jnp.sum(gh.astype(F32) * y - xh.astype(F32) * gin, axis=0, keepdims=True)
        return c

    lax.fori_loop(0, heads, head_step, 0)

    enter[:, mine_rows, :] = jnp.zeros((2, hrows, 128), F32)
    half_heads = pl.ds(pl.multiple_of(par * hh, hh), hh)
    rets = []
    for d in range(2):
        def gather(step, c, d=d):
            zz = step if d == 0 else pairs - 1 - step

            @pl.when(zz < pair if d == 0 else zz > pair)
            def _():
                pltpu.make_async_remote_copy(
                    src_ref=half.at[d], dst_ref=z_in.at[d, zz],
                    send_sem=z_send.at[d, zz], recv_sem=z_recv.at[d, zz],
                    device_id={"seq": 2 * zz + par}, device_id_type=MESH).wait_recv()
                ez = jnp.exp(tot[2 * zz, half_heads, :] + tot[2 * zz + 1, half_heads, :])
                for h in range(hh):
                    r = pl.ds(pl.multiple_of(par * hrows + h * hs, hs), hs)
                    enter[d, r, :] = ez[h:h + 1, :] * enter[d, r, :] + z_in[d, zz, h * hs:(h + 1) * hs, :].astype(F32)
            return c

        lax.fori_loop(0, pairs, gather, 0)
        for h in range(hh):
            r = pl.ds(pl.multiple_of(par * hrows + h * hs, hs), hs)
            lo, high = sides(d, h)
            base = enter[d, r, :]
            if d == 0:
                far = e_lo[h:h + 1, :] * base + lo
                far_mine = par == 1
            else:
                far = e_hi[h:h + 1, :] * base + high
                far_mine = par == 0
            enter[d, r, :] = jnp.where(far_mine, far, base)
            ret_out[d, h * hs:(h + 1) * hs, :] = jnp.where(far_mine, base, far).astype(BF16)
        c = to_mate(ret_out.at[d], ret_in.at[d], 2 + d)
        c.start()
        rets.append(c)
    rets[0].wait_recv()
    enter[0, mate_rows, :] = ret_in[0].astype(F32)
    for h in range(heads):
        r = slice(h * hs, (h + 1) * hs)
        state = enter[0, r, :]
        for b in range(blocks):
            nxt = e[b][h:h + 1, :] * state + fresh[b, r, :]
            fresh[b, r, :] = state
            state = nxt
        local[0, r, :] = state
    for b in range(blocks):
        t = slice(b * BLOCK, (b + 1) * BLOCK)
        qb = q_ref[t, :]
        sb = fresh[b].astype(BF16)
        mixed = jnp.where(rows >= cols, mixsum[b], 0.0).astype(BF16)
        gp_stage[0, t, :] = tn(mixed, qb)
        gp_stage[1, t, :] = nn(mixed, k_ref[t, :]) + tn(gs[b], sb)
        for h in range(heads):
            r = slice(h * hs, (h + 1) * hs)
            growth = jnp.exp(a_ref[b, h:h + 1, :])
            yc = nt(sb[r, :], qb)
            mis[b, h:h + 1, :] += jnp.sum(gt[b, r, :].astype(F32) * yc, axis=0, keepdims=True) * growth

    rets[1].wait_recv()
    enter[1, mate_rows, :] = ret_in[1].astype(F32)
    for h in range(heads):
        r = slice(h * hs, (h + 1) * hs)
        adj = enter[1, r, :]
        for b in reversed(range(blocks)):
            after = local[0, r, :] if b == blocks - 1 else fresh[b + 1, r, :]
            nxt = e[b][h:h + 1, :] * adj + up[b, r, :]
            base = jnp.sum(jnp.sum(after * adj, axis=0, keepdims=True), axis=1, keepdims=True)
            gd_ref[h:h + 1, b * BLOCK:(b + 1) * BLOCK] = jnp.broadcast_to(base, (1, BLOCK))
            up[b, r, :] = adj
            adj = nxt
    lower = (rows >= cols).astype(F32)
    for b in range(blocks):
        t = slice(b * BLOCK, (b + 1) * BLOCK)
        gp_stage[0, t, :] += tn(xs[b], up[b].astype(BF16))
    send_gp = to_head(gp_stage.at[other], gp_in, 2)
    send_gp.start()
    for b in range(blocks):
        t = slice(b * BLOCK, (b + 1) * BLOCK)
        kb = k_ref[t, :]
        for h in range(heads):
            r = slice(h * hs, (h + 1) * hs)
            arow = a_ref[b, h:h + 1, :]
            tail = jnp.exp(arow[:, BLOCK - 1:BLOCK] - arow)
            gc = nt(up[b, r, :].astype(BF16), kb) * tail
            gi[b, r, :] += gc
            mis[b, h:h + 1, :] -= jnp.sum(xt[b, r, :].astype(F32) * gc, axis=0, keepdims=True)
        gf_ref[t, :] = gi[b].astype(BF16).T
        gd_ref[:, t] += nn(mis[b], lower, precision=hi)
    send_gp.wait_recv()
    gp_ref[0] = gp_stage[hd] + gp_in[...]

    send_og.wait_send()
    send_w.wait_send()
    send_gp.wait_send()
    pair_f.wait_send()
    pair_b.wait_send()
    for d in range(2):
        rets[d].wait_send()
        z_each(d, lambda c: c.wait_send())

    def tot_done(j, c):
        @pl.when(j != me)
        def _():
            tot_copy(j).wait_send()
        return c

    lax.fori_loop(0, n, tot_done, 0)


def body(n, features, keys_proj, query_proj, log_decay, out_weight, out_grad):
    tokens, inner = features.shape
    heads = log_decay.shape[0]
    hs = inner // heads
    ns = keys_proj.shape[1]
    depth = out_grad.shape[1]
    blocks = tokens // BLOCK
    pairs = n // 2
    half = inner // 2
    vm = pltpu.VMEM
    dma = pltpu.SemaphoreType.DMA
    scratch = [
        vm((inner, depth), BF16), vm((tokens, depth), BF16), vm((tokens, ns), F32),
        vm((2, tokens, ns), F32), vm((n, heads, 128), F32),
        vm((2, inner, ns), BF16), vm((2, half, ns), BF16), vm((2, half, ns), BF16),
        vm((2, pairs, half, ns), BF16), vm((2, half, ns), BF16), vm((2, half, ns), BF16),
        vm((blocks, heads, BLOCK), F32), vm((blocks, heads, BLOCK, 1), F32),
        vm((blocks, inner, BLOCK), BF16), vm((blocks, inner, BLOCK), BF16),
        vm((blocks, inner, BLOCK), BF16), vm((blocks, inner, BLOCK), BF16),
        vm((blocks, inner, BLOCK), F32),
        vm((blocks, inner, ns), F32), vm((blocks, inner, ns), F32),
        vm((2, inner, ns), F32), vm((2, inner, ns), F32),
        vm((blocks, heads, BLOCK), F32), vm((blocks, BLOCK, BLOCK), F32), vm((blocks, BLOCK, BLOCK), F32),
        dma((3,)), dma((3,)), dma((n,)), dma((n,)), dma((4,)), dma((4,)),
        dma((2, pairs)), dma((2, pairs)),
    ]
    spec = pl.BlockSpec(memory_space=pltpu.VMEM)
    return pl.pallas_call(
        functools.partial(kernel, n, heads, hs, blocks),
        out_shape=(
            jax.ShapeDtypeStruct((tokens, inner), BF16),
            jax.ShapeDtypeStruct((1, tokens, ns), F32),
            jax.ShapeDtypeStruct((heads, tokens), F32),
        ),
        in_specs=[spec] * 6,
        out_specs=(spec,) * 3,
        scratch_shapes=scratch,
        compiler_params=pltpu.CompilerParams(
            collective_id=0, has_side_effects=True, vmem_limit_bytes=56 * 1024 * 1024),
    )(features, keys_proj, query_proj, log_decay, out_weight, out_grad)


def solution(mesh):
    placed = (
        P(("grp", "seq"), "head"),
        P(("grp", "seq"), None),
        P(("grp", "seq"), None),
        P("head", ("grp", "seq")),
        P(None, "head"),
        P(("grp", "seq"), "head"),
    )
    return jax.shard_map(
        functools.partial(body, mesh.shape["seq"]),
        mesh=mesh,
        in_specs=placed,
        out_specs=(
            P(("grp", "seq"), "head"),
            P("head", ("grp", "seq"), None),
            P("head", ("grp", "seq")),
        ),
        check_vma=False,
    )
```
